512 devices in a mesh: dp: 64 (over y, z_lo, core), tp: 8 (over x, z_hi).
Axes of the slice: x: 4, y: 8, z: 8 (z_hi: 2, z_lo: 4; z = z_hi * 4 + z_lo), core: 2. Of those that a mesh axis runs over, the one named last changes fastest.
Arguments:
- hidden: bfloat16 [4096, 5120], P('dp'), may hold values from -6 to 6
- norm_gain: float32 [5120], replicated, may hold values from 0.1 to 1.9
- w_query: bfloat16 [5120, 4096], P(('dp', 'tp')), may hold values from -0.078125 to 0.078125
- w_key: bfloat16 [5120, 1024], P(('dp', 'tp')), may hold values from -0.078125 to 0.078125
- w_value: bfloat16 [5120, 1024], P(('dp', 'tp')), may hold values from -0.078125 to 0.078125
- w_out: bfloat16 [4096, 5120], P(None, ('dp', 'tp')), may hold values from -0.09375 to 0.09375
- key_cache: bfloat16 [4096, 8, 128, 128], P('dp', 'tp'), may hold values from -136 to 136
- value_cache: bfloat16 [4096, 8, 128, 128], P('dp', 'tp'), may hold values from -6 to 6
- lengths: int32 [4096], P('dp'), may hold values from 1 to 128
- positions: int32 [4096], P('dp'), may hold values from 0 to 8190
Outputs:
- mixed: bfloat16 [4096, 5120], P('dp', 'tp')
The draws below stay inside these ranges and needn't reach their ends.
Inputs may be any that keep to these rules, and one draw needn't show every extreme that they name: `lengths`: slots at and beyond a row's length are not attended.
All inputs are finite; a program needn't handle non-finite values.
Results may differ from the reference program's by a relative error of at most 0.035.
The reference program's roundings to bfloat16 on the way (of `joined`, `h_one`, `att_one`, `middle` and `att_two`) count: a program that leaves them out, or rounds other values in their place, can miss the bound.
Values may be sent and summed in bfloat16 or wider, within the bound.
No kernel may reach another device: no remote copies, remote signals or barrier semaphores. Data moves between devices by JAX's collectives and lax.ppermute only.
A program may use at most 64 MiB of HBM per device.

```python
import math
import jax
import jax.numpy as jnp
from jax import lax

D = 5120
QH = 32
KVH = 8
HD = 128
CACHE = 128
ROWS_ALL = 4096
N_DP = 64


def draw_key_cache(key, part):
    key = jax.random.fold_in(key, 11)
    shape = (ROWS_ALL, KVH, CACHE, HD)
    values = jnp.clip(jax.random.normal(key, shape, jnp.float32), -6.0, 6.0)
    return values.astype(jnp.bfloat16)


def touch_ends(array, rng, low, top_value):
    spot = [jax.random.randint(jax.random.fold_in(rng, axis), (), 0, length) for axis, length in enumerate(array.shape)]
    widest = array.shape.index(max(array.shape))
    beside = spot[:widest] + [(spot[widest] + 1) % array.shape[widest]] + spot[widest + 1:]
    return array.at[tuple(spot)].set(low).at[tuple(beside)].set(top_value)


def steps_of(stream_key, extent, cuts, least, top_value):
    level, own = 1.0, jax.random.fold_in(stream_key, 6)
    for position, shards_of in cuts:
        draws = jnp.exp(jax.random.uniform(jax.random.fold_in(own, position), (shards_of,), jnp.float32, least / len(cuts), top_value / len(cuts)))
        level = level * jnp.repeat(draws, extent[position] // shards_of).reshape([-1 if axis == position else 1 for axis in range(len(extent))])
    return level


def bell_draw(stream_key, dims, width, reach, pieces=(), kind=jnp.bfloat16):
    drawn = jax.random.normal(stream_key, dims, jnp.float32) * width
    if len(pieces) > 0:
        drawn = steps_of(stream_key, dims, pieces, -0.22, 0.18) * drawn
    return jnp.clip(drawn, min=-reach, max=reach).astype(kind)


def setup_inputs(seed: int = 0) -> dict:
    seeds = jax.random.split(jax.random.key(seed), 11)
    return {
        "hidden": bell_draw(seeds[0], (ROWS_ALL, D), 1.0, 6.0, ((0, 64),)),
        "norm_gain": jnp.clip(1.0 + 0.18 * jax.random.normal(seeds[1], (D,), jnp.float32), 0.1, 1.9),
        "w_query": bell_draw(seeds[2], (D, QH * HD), D ** -0.5, 0.078125, ((0, 512),)),
        "w_key": bell_draw(seeds[3], (D, KVH * HD), D ** -0.5, 0.078125, ((0, 512),)),
        "w_value": bell_draw(seeds[4], (D, KVH * HD), D ** -0.5, 0.078125, ((0, 512),)),
        "w_out": bell_draw(seeds[5], (QH * HD, D), (QH * HD) ** -0.5, 0.09375, ((1, 512),)),
        "key_cache": draw_key_cache(jax.random.fold_in(seeds[10], 71), 0),
        "value_cache": bell_draw(seeds[7], (ROWS_ALL, KVH, CACHE, HD), 1.0, 6.0, ((0, 64), (1, 8))),
        "lengths": touch_ends(jax.random.randint(seeds[8], (ROWS_ALL,), 1, CACHE + 1), jax.random.fold_in(seeds[8], 1), 1, CACHE).astype(jnp.int32),
        "positions": touch_ends(jax.random.randint(seeds[9], (ROWS_ALL,), 0, 8191), jax.random.fold_in(seeds[9], 1), 0, 8190).astype(jnp.int32),
    }


THETA = 1000000.0
EPS = 1e-06

def rotate(vectors, token_pos):
    half_dim = vectors.shape[-1] // 2
    inverse = jnp.exp(jnp.arange(half_dim).astype(jnp.float32) * (-2.0 * math.log(THETA) / vectors.shape[-1]))
    angles = token_pos.astype(jnp.float32)[:, None] * inverse[None, :]
    cosine = jnp.cos(angles)[:, None, :]
    sine = jnp.sin(angles)[:, None, :]
    front = vectors[..., :half_dim]
    back = vectors[..., half_dim:]
    return jnp.concatenate([front * cosine - back * sine, back * cosine + front * sine], axis=-1)

def rms_norm(values, gain):
    widened = values.astype(jnp.float32)
    factor = lax.rsqrt(lax.optimization_barrier(jnp.mean(widened * widened, axis=1, keepdims=True)) + EPS)
    return (widened * factor * gain).astype(jnp.bfloat16)

def heads_of(product, token_pos, q_width, kv_width, kv_heads):
    row_count = product.shape[0]
    queries = rotate(product[:, :q_width].reshape(row_count, q_width // HD, HD), token_pos).astype(jnp.bfloat16)
    queries = queries.reshape(row_count, kv_heads, q_width // HD // kv_heads, HD)
    keys_new = rotate(product[:, q_width:q_width + kv_width].reshape(row_count, kv_heads, HD), token_pos).astype(jnp.bfloat16)
    values_new = product[:, q_width + kv_width:].astype(jnp.bfloat16).reshape(row_count, kv_heads, HD)
    return (queries, keys_new, values_new)

def attend(queries, key_cache, value_cache, lengths, new_keys, new_values):
    all_keys = jnp.concatenate([key_cache, new_keys], axis=2).astype(jnp.float32)
    all_values = jnp.concatenate([value_cache, new_values], axis=2).astype(jnp.float32)
    slots = jnp.arange(all_keys.shape[2])
    valid = (slots[None, :] < lengths[:, None]) | (slots[None, :] >= key_cache.shape[2])
    scores = jnp.einsum('rhgd,rhld->rhgl', queries.astype(jnp.float32), all_keys) * queries.shape[-1] ** (-0.5)
    scores = jnp.where(valid[:, None, None, :], scores, -1e+30)
    highest = lax.optimization_barrier(jnp.max(scores, axis=-1, keepdims=True))
    weights = jnp.exp(scores - highest)
    weights = (weights / lax.optimization_barrier(jnp.sum(weights, axis=-1, keepdims=True))).astype(jnp.bfloat16)
    summed = jnp.einsum('rhgl,rhld->rhgd', weights.astype(jnp.float32), all_values)
    return summed.astype(jnp.bfloat16).reshape(queries.shape[0], -1)

def grouped(queries, key_cache, value_cache, lengths, new_keys, new_values):

    def split_up(member):
        return member.reshape((N_DP, member.shape[0] // N_DP) + member.shape[1:])

    def run_block(items):
        return attend(items[0], items[1], items[2], items[3], items[4], items[5])
    blocks = tuple((split_up(member) for member in (queries, key_cache, value_cache, lengths, new_keys, new_values)))
    outputs = lax.map(run_block, blocks)
    return outputs.reshape(queries.shape[0], -1)

def reference(hidden, norm_gain, w_query, w_key, w_value, w_out, key_cache, value_cache, lengths, positions):
    joined = jnp.concatenate([w_query, w_key, w_value], axis=1)
    q_width = w_query.shape[1]
    kv_width = w_key.shape[1]
    h_one = rms_norm(hidden, norm_gain)
    query_one, key_one, value_one = heads_of(jnp.dot(h_one, joined, preferred_element_type=jnp.float32), positions, q_width, kv_width, KVH)
    att_one = grouped(query_one, key_cache, value_cache, lengths, key_one[:, :, None], value_one[:, :, None])
    middle = (hidden.astype(jnp.float32) + jnp.dot(att_one, w_out, preferred_element_type=jnp.float32)).astype(jnp.bfloat16)
    h_two = rms_norm(middle, norm_gain)
    query_two, key_two, value_two = heads_of(jnp.dot(h_two, joined, preferred_element_type=jnp.float32), positions + 1, q_width, kv_width, KVH)
    att_two = grouped(query_two, key_cache, value_cache, lengths, jnp.stack([key_one, key_two], axis=2), jnp.stack([value_one, value_two], axis=2))
    return (middle.astype(jnp.float32) + jnp.dot(att_two, w_out, preferred_element_type=jnp.float32)).astype(jnp.bfloat16)
```

```python
import math

import jax
import jax.numpy as jnp
from jax import lax
from jax.sharding import PartitionSpec as P

HD = 128


THETA = 1000000.0
EPS = 1e-06


def rotate(vectors, token_pos):
    half_dim = vectors.shape[-1] // 2
    inverse = jnp.exp(
        jnp.arange(half_dim).astype(jnp.float32) * (-2.0 * math.log(THETA) / vectors.shape[-1])
    )
    angles = token_pos.astype(jnp.float32)[:, None] * inverse[None, :]
    cosine = jnp.cos(angles)[:, None, :]
    sine = jnp.sin(angles)[:, None, :]
    front = vectors[..., :half_dim]
    back = vectors[..., half_dim:]
    return jnp.concatenate([front * cosine - back * sine, back * cosine + front * sine], axis=-1)


def rms_norm(values, gain):
    widened = values.astype(jnp.float32)
    factor = lax.rsqrt(jnp.mean(widened * widened, axis=1, keepdims=True) + EPS)
    return (widened * factor * gain).astype(jnp.bfloat16)


def heads_of(product, token_pos, q_width, kv_width, kv_heads):
    row_count = product.shape[0]
    queries = rotate(product[:, :q_width].reshape(row_count, q_width // HD, HD), token_pos).astype(
        jnp.bfloat16
    )
    queries = queries.reshape(row_count, kv_heads, q_width // HD // kv_heads, HD)
    keys_new = rotate(
        product[:, q_width : q_width + kv_width].reshape(row_count, kv_heads, HD), token_pos
    ).astype(jnp.bfloat16)
    values_new = (
        product[:, q_width + kv_width :].astype(jnp.bfloat16).reshape(row_count, kv_heads, HD)
    )
    return (queries, keys_new, values_new)


def attend(queries, key_cache, value_cache, lengths, new_keys, new_values):
    all_keys = jnp.concatenate([key_cache, new_keys], axis=2)
    all_values = jnp.concatenate([value_cache, new_values], axis=2)
    slots = jnp.arange(all_keys.shape[2])
    valid = (slots[None, :] < lengths[:, None]) | (slots[None, :] >= key_cache.shape[2])
    scores = jnp.einsum(
        "rhgd,rhld->rhgl", queries, all_keys, preferred_element_type=jnp.float32
    ) * queries.shape[-1] ** (-0.5)
    scores = jnp.where(valid[:, None, None, :], scores, -1e30)
    highest = jnp.max(scores, axis=-1, keepdims=True)
    weights = jnp.exp(scores - highest)
    weights = (weights / jnp.sum(weights, axis=-1, keepdims=True)).astype(jnp.bfloat16)
    summed = jnp.einsum("rhgl,rhld->rhgd", weights, all_values, preferred_element_type=jnp.float32)
    return summed.astype(jnp.bfloat16).reshape(queries.shape[0], -1)


def on_device(
    hidden, norm_gain, w_query, w_key, w_value, w_out, key_cache, value_cache, lengths, positions
):
    tp_count = lax.axis_size("tp")
    tp_rank = lax.axis_index("tp")
    rows, model_width = hidden.shape
    kv_local = key_cache.shape[1]
    q_width = w_query.shape[1] // tp_count
    kv_width = w_key.shape[1] // tp_count
    share_width = model_width // tp_count
    col_start = tp_rank * share_width

    def by_slice(flat):
        return flat.reshape(flat.shape[0], tp_count, -1).transpose(1, 0, 2)

    packed = jnp.concatenate(
        [by_slice(w_query), by_slice(w_key), by_slice(w_value), by_slice(w_out.T)], axis=2
    )
    packed = lax.all_to_all(packed, "tp", split_axis=0, concat_axis=0, tiled=True)
    packed = packed.reshape(-1, packed.shape[2])
    gathered = lax.all_gather(packed, "dp", axis=0, tiled=True)
    slice_weight = gathered[:, : q_width + 2 * kv_width]
    out_weight = gathered[:, q_width + 2 * kv_width :].T

    def sum_over_heads(partial):
        blocks = partial.astype(jnp.bfloat16).reshape(rows, tp_count, share_width)
        blocks = lax.all_to_all(
            blocks.transpose(1, 0, 2), "tp", split_axis=0, concat_axis=0, tiled=True
        )
        return jnp.sum(blocks.astype(jnp.float32), axis=0)

    hidden_share = lax.dynamic_slice_in_dim(hidden, col_start, share_width, 1)
    h_one = rms_norm(hidden, norm_gain)
    product_one = jnp.dot(h_one, slice_weight, preferred_element_type=jnp.float32)
    query_one, key_one, value_one = heads_of(product_one, positions, q_width, kv_width, kv_local)
    att_one = attend(
        query_one, key_cache, value_cache, lengths, key_one[:, :, None], value_one[:, :, None]
    )
    partial_one = jnp.dot(att_one, out_weight, preferred_element_type=jnp.float32)
    middle_share = (hidden_share.astype(jnp.float32) + sum_over_heads(partial_one)).astype(
        jnp.bfloat16
    )
    middle = lax.all_to_all(
        jnp.broadcast_to(middle_share[None], (tp_count, rows, share_width)),
        "tp",
        split_axis=0,
        concat_axis=0,
        tiled=True,
    )
    middle = middle.transpose(1, 0, 2).reshape(rows, model_width)
    h_two = rms_norm(middle, norm_gain)
    product_two = jnp.dot(h_two, slice_weight, preferred_element_type=jnp.float32)
    query_two, key_two, value_two = heads_of(
        product_two, positions + 1, q_width, kv_width, kv_local
    )
    att_two = attend(
        query_two,
        key_cache,
        value_cache,
        lengths,
        jnp.stack([key_one, key_two], axis=2),
        jnp.stack([value_one, value_two], axis=2),
    )
    partial_two = jnp.dot(att_two, out_weight, preferred_element_type=jnp.float32)
    final_share = sum_over_heads(partial_two)
    return (middle_share.astype(jnp.float32) + final_share).astype(jnp.bfloat16)


def solution(mesh):
    return jax.shard_map(
        on_device,
        mesh=mesh,
        in_specs=(
            P("dp", None),
            P(),
            P(("dp", "tp"), None),
            P(("dp", "tp"), None),
            P(("dp", "tp"), None),
            P(None, ("dp", "tp")),
            P("dp", "tp", None, None),
            P("dp", "tp", None, None),
            P("dp"),
            P("dp"),
        ),
        out_specs=P("dp", "tp"),
        check_vma=False,
    )
```
